512 devices in a mesh: prompt: 8 (over x, z_hi), trainer: 16 (over z_lo, core), tensor: 4 (over y).
Axes of the slice: x: 4, y: 4, z: 16 (z_hi: 2, z_lo: 8; z = z_hi * 8 + z_lo), core: 2. Of those that a mesh axis runs over, the one named last changes fastest.
Arguments:
- queries: bfloat16 [8, 16, 256, 2560], P('prompt', 'trainer', None, 'tensor'), may hold values from -72 to 72
- resp_keys: bfloat16 [8, 16, 256, 512], P('prompt', 'trainer', None, 'tensor'), may hold values from -72 to 72
- resp_values: bfloat16 [8, 16, 256, 512], P('prompt', 'trainer', None, 'tensor'), may hold values from -6 to 6
- prompt_keys: bfloat16 [8, 512, 512], P('prompt', 'trainer', 'tensor'), may hold values from -6 to 6
- prompt_values: bfloat16 [8, 512, 512], P('prompt', 'trainer', 'tensor'), may hold values from -6 to 6
- q_gain: float32 [2560], P('tensor'), may hold values from 1 to 3
- k_gain: float32 [512], P('tensor'), may hold values from 1 to 3
- lengths: int32 [8, 16], P('prompt', 'trainer'), may hold values from 1 to 256, 2048 in all within a row
- block_rank: int32 [8, 16, 2], P('prompt'), may hold values from 0 to 15, as said below
- out_grad: bfloat16 [8, 16, 256, 2560], P('prompt', 'trainer', None, 'tensor'), may hold values from -6 to 6
Outputs:
- attn_out: bfloat16 [8, 16, 256, 2560], P('prompt', 'trainer', None, 'tensor')
- grad_queries: bfloat16 [8, 16, 256, 2560], P('prompt', 'trainer', None, 'tensor')
- grad_keys: bfloat16 [8, 16, 256, 512], P('prompt', 'trainer', None, 'tensor')
- grad_values: bfloat16 [8, 16, 256, 512], P('prompt', 'trainer', None, 'tensor')
- grad_prompt_keys: bfloat16 [8, 512, 512], P('prompt', 'trainer', 'tensor')
- grad_prompt_values: bfloat16 [8, 512, 512], P('prompt', 'trainer', 'tensor')
- grad_q_gain: float32 [2560], P('tensor')
- grad_k_gain: float32 [512], P('tensor')
The draws below stay inside these ranges and needn't reach their ends.
Inputs may be any that keep to these rules, and one draw needn't show every extreme that they name: In each group the 16 response lengths sum to 2048, and the longest is 256. Block b of the response at trainer index t of group g goes to slot b of rank block_rank[g, t, b]. For each g and b the ranks over t are a permutation of the 16 ranks, and the 2 blocks of one response go to different ranks.
All inputs are finite; a program needn't handle non-finite values.
Results may differ from the reference program's by a relative error of at most 0.018.
The reference program's roundings to bfloat16 on the way count: a program that leaves them out, or rounds other values in their place, can miss the bound.
Values may be sent and summed in bfloat16 or wider, within the bound.
No kernel may reach another device: no remote copies, remote signals or barrier semaphores. Data moves between devices by JAX's collectives and lax.ppermute only.
A program may use at most 64 MiB of HBM per device.

```python
import math
import jax
import jax.numpy as jnp
import numpy as np
from jax import lax

HEAD = 128
HEADS = 20
KV_HEADS = 4
BLOCK = 128
BLOCKS = 2
RESP = 256
PROMPT = 512
N_PROMPT = 8
N_TRAINER = 16


def draw_queries(key, part):
    key = jax.random.fold_in(key, 11)
    key_base = jax.random.fold_in(key, 0)
    array_shape = (N_PROMPT, N_TRAINER, RESP, HEADS, HEAD)
    sample = jnp.clip(jax.random.normal(key_base, array_shape, jnp.float32), -6.0, 6.0)
    return sample.reshape(N_PROMPT, N_TRAINER, RESP, HEADS * HEAD).astype(jnp.bfloat16)


def draw_resp_keys(key, part):
    key = jax.random.fold_in(key, 37)
    key_base = jax.random.fold_in(key, 0)
    array_shape = (N_PROMPT, N_TRAINER, RESP, KV_HEADS, HEAD)
    sample = jnp.clip(jax.random.normal(key_base, array_shape, jnp.float32), -6.0, 6.0)
    return sample.reshape(N_PROMPT, N_TRAINER, RESP, KV_HEADS * HEAD).astype(jnp.bfloat16)


def draw_prompt_keys(key, part):
    key = jax.random.fold_in(key, 23)
    array_shape = (N_PROMPT, PROMPT, KV_HEADS, HEAD)
    sample = jnp.clip(jax.random.normal(key, array_shape, jnp.float32), -6.0, 6.0)
    return sample.reshape(N_PROMPT, PROMPT, KV_HEADS * HEAD).astype(jnp.bfloat16)


def draw_block_rank(key, part):
    key = jax.random.fold_in(key, 51)
    group_keys = jax.random.split(key, N_PROMPT)

    def draw_group(group_key):
        key_order, key_start, key_offset = jax.random.split(group_key, 3)
        rank_order = jax.random.permutation(key_order, N_TRAINER)
        start_order = jax.random.permutation(key_start, N_TRAINER)
        offsets = jax.random.permutation(key_offset, N_TRAINER)[:BLOCKS]
        position = (start_order[:, None] + offsets[None, :]) % N_TRAINER
        return rank_order[position].astype(jnp.int32)
    return jax.vmap(draw_group)(group_keys)


def block_levels(rng, dims, cuts, smallest, largest):
    loudness = 1.0
    for dim, parts in cuts:
        heights = jax.random.uniform(jax.random.fold_in(jax.random.fold_in(rng, 6), dim), (parts,), jnp.float32, smallest / len(cuts), largest / len(cuts))
        loudness = loudness * jnp.repeat(jnp.exp(heights), dims[dim] // parts).reshape((-1,) + (1,) * (len(dims) - 1 - dim))
    return loudness


def profile(count, total, limit, skew):
    weights = [(1 << 20) // math.isqrt(grade ** skew) + 1 for grade in range(2, count + 1)]
    surplus, counts = total - limit - (count - 1), [1] * (count - 1)
    while surplus > 0:
        candidates = [i for i in range(count - 1) if counts[i] < limit]
        mass, left = sum([weights[i] for i in candidates]), surplus
        for i in candidates:
            more = min(limit - counts[i], max(1, left * weights[i] // mass), surplus)
            counts[i] = counts[i] + more
            surplus = surplus - more
    return np.array([limit] + counts)


def uneven(key, amount, total, bound, lean):
    if amount == 2:
        one = jax.random.randint(key, (), max(1, total - bound), min(bound, total - 1) + 1)
        return jnp.stack([one, total - one])
    sizes = jnp.asarray(profile(amount, total, bound, lean), jnp.int32)
    couples = (amount - 1) // 2
    giver, taker = sizes[1:1 + 2 * couples:2], sizes[2:2 + 2 * couples:2]
    margin = jnp.minimum(giver - 1, bound - taker)
    shifted = jax.random.randint(jax.random.fold_in(key, 1), (couples,), 0, 1 << 20) % (margin + 1)
    sizes = sizes.at[1:1 + 2 * couples:2].set(giver - shifted).at[2:2 + 2 * couples:2].set(taker + shifted)
    return sizes[jax.random.permutation(jax.random.fold_in(key, 2), amount)]


def scatter_about(rng, shape, deviation, most, cuts=(), kind=jnp.bfloat16):
    entries = deviation * jax.random.normal(rng, shape, jnp.float32)
    if cuts:
        entries = entries * block_levels(rng, shape, cuts, -0.22, 0.18)
    return jnp.clip(entries, -most, most).astype(kind)


def setup_inputs(seed: int = 0) -> dict:
    splits = jax.random.split(jax.random.key(seed), 11)
    return {
        "queries": draw_queries(jax.random.fold_in(splits[10], 71), 0),
        "resp_keys": draw_resp_keys(jax.random.fold_in(splits[10], 71), 0),
        "resp_values": scatter_about(splits[2], (N_PROMPT, N_TRAINER, RESP, KV_HEADS * HEAD), 1.0, 6.0, ((0, 8), (1, 16), (3, 4))),
        "prompt_keys": draw_prompt_keys(jax.random.fold_in(splits[10], 71), 0),
        "prompt_values": scatter_about(splits[4], (N_PROMPT, PROMPT, KV_HEADS * HEAD), 1.0, 6.0, ((0, 8), (1, 16), (2, 4))),
        "q_gain": jnp.clip(jnp.exp(math.log(3.0) - 1.0986123 * jax.random.uniform(splits[5], (HEADS * HEAD,), jnp.float32) ** block_levels(splits[5], (HEADS * HEAD,), ((0, 4),), -0.2, 0.2)), 1.0, 3.0),
        "k_gain": jnp.clip(jnp.exp(math.log(3.0) - 1.0986123 * jax.random.uniform(splits[6], (KV_HEADS * HEAD,), jnp.float32) ** block_levels(splits[6], (KV_HEADS * HEAD,), ((0, 4),), -0.2, 0.2)), 1.0, 3.0),
        "lengths": jax.vmap(lambda own: uneven(own, N_TRAINER, N_TRAINER * RESP // 2, RESP, 2))(jax.random.split(splits[7], N_PROMPT)).reshape((N_PROMPT, N_TRAINER)).astype(jnp.int32),
        "block_rank": draw_block_rank(jax.random.fold_in(splits[10], 71), 0),
        "out_grad": scatter_about(splits[9], (N_PROMPT, N_TRAINER, RESP, HEADS * HEAD), 1.0, 6.0, ((0, 8), (1, 16), (3, 4))),
    }


epsilon = 1e-06

def widen(array):
    return lax.optimization_barrier(array).astype(jnp.float32)

def norm_rows(raw, gain):
    raw_float = raw.astype(jnp.float32)
    factor = lax.rsqrt(lax.optimization_barrier(jnp.mean(raw_float * raw_float, axis=-1, keepdims=True)) + epsilon)
    normed = raw_float * factor
    return (normed, factor, (normed * gain).astype(jnp.bfloat16))

def norm_back(grad_normed, normed, factor, gain):
    inner_grad = grad_normed * gain
    mixing = lax.optimization_barrier(jnp.mean(inner_grad * normed, axis=-1, keepdims=True))
    return ((factor * (inner_grad - normed * mixing)).astype(jnp.bfloat16), lax.optimization_barrier(jnp.sum(grad_normed * normed, axis=0)))

def home_pass(query_raw, key_raw, value_raw, prompt_key, prompt_value, q_gain, k_gain, length, grad_out):
    row_count = query_raw.shape[0]
    group_size = HEADS // KV_HEADS
    normed_query, query_factor, query_n = norm_rows(query_raw, q_gain)
    normed_key, key_factor, key_n = norm_rows(key_raw, k_gain)
    key_list = widen(jnp.concatenate([prompt_key, key_n], axis=0)).reshape(PROMPT + row_count, KV_HEADS, HEAD)
    value_list = jnp.concatenate([prompt_value, value_raw], axis=0).astype(jnp.float32).reshape(PROMPT + row_count, KV_HEADS, HEAD)
    query_four = widen(query_n).reshape(row_count, KV_HEADS, group_size, HEAD)
    score_scale = HEAD ** (-0.5)
    raw_scores = jnp.einsum('rkge,jke->kgrj', query_four, key_list) * score_scale
    query_pos = jnp.arange(row_count, dtype=jnp.int32)[:, None]
    key_pos = jnp.arange(PROMPT + row_count, dtype=jnp.int32)[None, :] - PROMPT
    allowed = (key_pos < 0) | (key_pos <= query_pos) & (key_pos < length)
    scores = jnp.where(allowed, raw_scores, -1e+30)
    row_max = lax.optimization_barrier(jnp.max(scores, axis=-1, keepdims=True))
    log_total = row_max + jnp.log(lax.optimization_barrier(jnp.sum(jnp.exp(scores - row_max), axis=-1, keepdims=True)))
    weights = jnp.exp(scores - log_total)
    weights_half = widen(weights.astype(jnp.bfloat16))
    live = jnp.arange(row_count, dtype=jnp.int32) < length
    attended = jnp.einsum('kgrj,jke->rkge', weights_half, value_list) * live.astype(jnp.float32)[:, None, None, None]
    attended = attended.astype(jnp.bfloat16)
    grad_live = grad_out * live.astype(jnp.bfloat16)[:, None]
    grad_four = widen(grad_live).reshape(row_count, KV_HEADS, group_size, HEAD)
    row_inner = lax.optimization_barrier(jnp.sum(grad_four * widen(attended), axis=-1))
    prob_grad = jnp.einsum('rkge,jke->kgrj', grad_four, value_list)
    score_grad = weights * (prob_grad - jnp.transpose(row_inner, (1, 2, 0))[..., None]) * score_scale
    score_half = widen(score_grad.astype(jnp.bfloat16))
    grad_query = jnp.einsum('kgrj,jke->rkge', score_half, key_list).reshape(row_count, HEADS * HEAD)
    grad_keylist = jnp.einsum('kgrj,rkge->jke', score_half, query_four).reshape(PROMPT + row_count, KV_HEADS * HEAD)
    grad_valuelist = jnp.einsum('kgrj,rkge->jke', weights_half, grad_four).reshape(PROMPT + row_count, KV_HEADS * HEAD)
    grad_queries, query_gain_term = norm_back(grad_query, normed_query, query_factor, q_gain)
    grad_keys, key_gain_term = norm_back(grad_keylist[PROMPT:], normed_key, key_factor, k_gain)
    return (attended.reshape(row_count, HEADS * HEAD), grad_queries, grad_keys, grad_valuelist[PROMPT:].astype(jnp.bfloat16), grad_keylist[:PROMPT], grad_valuelist[:PROMPT], query_gain_term, key_gain_term)

def reference(queries, resp_keys, resp_values, prompt_keys, prompt_values, q_gain, k_gain, lengths, block_rank, out_grad):
    group_index = jnp.arange(N_PROMPT, dtype=jnp.int32)[:, None, None]
    slot_index = jnp.arange(BLOCKS, dtype=jnp.int32)[None, None, :]
    rank_index = block_rank.astype(jnp.int32)
    grad_blocks = out_grad.reshape(N_PROMPT, N_TRAINER, BLOCKS, BLOCK, HEADS * HEAD)
    grad_home = grad_blocks[group_index, rank_index, slot_index].reshape(N_PROMPT, N_TRAINER, RESP, HEADS * HEAD)

    def group_pass(bundled):
        query_group, key_group, value_group, prompt_key, prompt_value, length_group, grad_group = bundled

        def home_step(carried, home_data):
            query_raw, key_raw, value_raw, length, grad_out = home_data
            results = home_pass(query_raw, key_raw, value_raw, prompt_key, prompt_value, q_gain, k_gain, length, grad_out)
            carried = (carried[0] + results[4], carried[1] + results[5], carried[2] + results[6], carried[3] + results[7])
            return (carried, results[:4])
        initial = (jnp.zeros((PROMPT, KV_HEADS * HEAD), jnp.float32), jnp.zeros((PROMPT, KV_HEADS * HEAD), jnp.float32), jnp.zeros((HEADS * HEAD,), jnp.float32), jnp.zeros((KV_HEADS * HEAD,), jnp.float32))
        carried, stacked = lax.scan(home_step, initial, (query_group, key_group, value_group, length_group, grad_group))
        return stacked + (carried[0].astype(jnp.bfloat16), carried[1].astype(jnp.bfloat16), carried[2], carried[3])
    outputs = lax.map(group_pass, (queries, resp_keys, resp_values, prompt_keys, prompt_values, lengths, grad_home))
    attended, grad_queries, grad_keys, grad_values, grad_prompt_keys, grad_prompt_values, query_terms, key_terms = outputs
    attended_blocks = attended.reshape(N_PROMPT, N_TRAINER, BLOCKS, BLOCK, HEADS * HEAD)
    placed = jnp.zeros_like(attended_blocks).at[group_index, rank_index, slot_index].set(attended_blocks)
    return (placed.reshape(N_PROMPT, N_TRAINER, RESP, HEADS * HEAD), grad_queries, grad_keys, grad_values, grad_prompt_keys, grad_prompt_values, lax.optimization_barrier(jnp.sum(query_terms, axis=0)), lax.optimization_barrier(jnp.sum(key_terms, axis=0)))
```

```python
import jax
import jax.numpy as jnp
from jax import lax
from jax.experimental import pallas as pl
from jax.experimental.pallas import tpu as pltpu
from jax.sharding import PartitionSpec as P

HEAD = 128
HEADS = 20
KV_HEADS = 4
GROUP = HEADS // KV_HEADS
BLOCK = 128
BLOCKS = 2
RESP = BLOCK * BLOCKS
PROMPT = 512
KEYS = PROMPT + RESP
CHUNKS = KEYS // BLOCK
PROMPT_CHUNKS = PROMPT // BLOCK
N_TRAINER = 16
N_TENSOR = 4
PROMPTS = ("x", "zhi")
TRAINER = ("zlo", "core")
WIDTH = GROUP * HEAD
GAIN_ROWS = (GROUP + 1) // 2
SCALE = HEAD ** (-0.5)

epsilon = 1e-06
f32 = jnp.float32
bf16 = jnp.bfloat16

PARAMS = pltpu.CompilerParams(vmem_limit_bytes=24 * 1024 * 1024)
VMEM = pl.BlockSpec(memory_space=pltpu.VMEM)
SMEM = pl.BlockSpec(memory_space=pltpu.SMEM)


def nt(left, right):
    return lax.dot_general(left, right, (((1,), (1,)), ((), ())), preferred_element_type=f32)


def nn(left, right):
    return jnp.dot(left, right, preferred_element_type=f32)


def columns_to_tile(columns):
    wide = [jnp.broadcast_to(c, (BLOCK, BLOCK)).T[:1] for c in columns]
    wide.append(jnp.zeros((8 - len(columns), BLOCK), f32))
    return jnp.concatenate(wide, axis=0)


def tile_to_columns(tile):
    turned = jnp.concatenate([tile] * (BLOCK // 8), axis=0).T
    first = jnp.concatenate([turned[:, 0:1], turned[:, 1:2]], axis=0)
    second = jnp.concatenate([turned[:, 2:3], turned[:, 3:4]], axis=0)
    return first, second


def factors(sums_ref):
    total = sums_ref[0]
    for i in range(1, N_TENSOR):
        total = total + sums_ref[i]
    query_sums, key_sums = tile_to_columns(total)
    query_factor = lax.rsqrt(query_sums / (HEADS * HEAD) + epsilon)
    key_factor = lax.rsqrt(key_sums / (KV_HEADS * HEAD) + epsilon)
    return query_factor, key_factor


def stats_kernel(q_ref, k_ref, pk_ref, pv_ref, sums_ref, kv_ref):
    raw_query = q_ref[...].astype(f32)
    raw_key = k_ref[...].astype(f32)
    query_sums = jnp.sum(raw_query * raw_query, axis=1, keepdims=True)
    key_sums = jnp.sum(raw_key * raw_key, axis=1, keepdims=True)
    tile = columns_to_tile(
        [query_sums[:BLOCK], query_sums[BLOCK:], key_sums[:BLOCK], key_sums[BLOCK:]]
    )
    for i in range(N_TENSOR):
        sums_ref[i] = tile
    pair = jnp.concatenate([pk_ref[...], pv_ref[...]], axis=1)
    for i in range(N_TRAINER):
        kv_ref[i] = pair


def masked(scores, chunk, length):
    if chunk < PROMPT_CHUNKS:
        return scores
    key_pos = lax.broadcasted_iota(jnp.int32, scores.shape, 0) + (chunk - PROMPT_CHUNKS) * BLOCK
    query_pos = lax.broadcasted_iota(jnp.int32, scores.shape, 1)
    return jnp.where((key_pos <= query_pos) & (key_pos < length), scores, -1e30)


def live_column(length):
    rows = lax.broadcasted_iota(jnp.int32, (RESP, 1), 0)
    return (rows < length).astype(f32)


def forward_kernel(
    info_ref, q_ref, k_ref, v_ref, kv_ref, sums_ref, qg_ref, kg_ref,
    qn_ref, keys_ref, lse_ref, out_ref,
    values_t_ref, s_ref, p_ref,
):
    length = info_ref[0]
    query_factor, key_factor = factors(sums_ref)
    qn_ref[...] = (q_ref[...].astype(f32) * query_factor * qg_ref[...]).astype(bf16)
    keys_ref[:PROMPT] = kv_ref[:, :HEAD]
    keys_ref[PROMPT:] = (k_ref[...].astype(f32) * key_factor * kg_ref[...]).astype(bf16)
    values_t_ref[:, :PROMPT] = kv_ref[:, HEAD:].astype(f32).T.astype(bf16)
    values_t_ref[:, PROMPT:] = v_ref[...].astype(f32).T.astype(bf16)
    live = live_column(length)
    for h in range(GROUP):
        cols = slice(h * HEAD, (h + 1) * HEAD)
        query = qn_ref[:, cols]
        top = None
        for c in range(CHUNKS):
            rows = slice(c * BLOCK, (c + 1) * BLOCK)
            scores = masked(nt(keys_ref[rows], query) * SCALE, c, length)
            s_ref[rows] = scores
            most = jnp.max(scores, axis=0, keepdims=True)
            top = most if top is None else jnp.maximum(top, most)
        total = jnp.zeros_like(top)
        for c in range(CHUNKS):
            rows = slice(c * BLOCK, (c + 1) * BLOCK)
            grown = jnp.exp(s_ref[rows] - top)
            s_ref[rows] = grown
            total = total + jnp.sum(grown, axis=0, keepdims=True)
        share = 1.0 / total
        for c in range(CHUNKS):
            rows = slice(c * BLOCK, (c + 1) * BLOCK)
            p_ref[rows] = (s_ref[rows] * share).astype(bf16)
        lse_ref[h : h + 1] = top + jnp.log(total)
        attended = nn(values_t_ref[...], p_ref[...]).T
        out_ref[:, cols] = (attended * live).astype(bf16)
    lse_ref[GROUP:] = jnp.zeros((8 - GROUP, RESP), f32)


def backward_kernel(
    info_ref, q_ref, k_ref, v_ref, kv_ref, sums_ref, qg_ref, kg_ref,
    qn_ref, keys_ref, lse_ref, out_ref, own_ref, passed_ref,
    u_ref, w_ref, gv_ref, terms_ref, mix_ref, gain_ref,
    keys_t_ref, grad_ref, ds_ref, dk_ref, dv_ref,
):
    length = info_ref[0]
    query_factor, key_factor = factors(sums_ref)
    keys_t_ref[...] = keys_ref[...].astype(f32).T.astype(bf16)
    live = live_column(length).astype(bf16)
    swapped = info_ref[1] != 0
    first = jnp.where(swapped, passed_ref[...], own_ref[...])
    second = jnp.where(swapped, own_ref[...], passed_ref[...])
    grad_ref[:BLOCK] = first * live[:BLOCK]
    grad_ref[BLOCK:] = second * live[BLOCK:]
    query_mix = jnp.zeros((RESP, 1), f32)
    gain_rows = []
    for h in range(GROUP):
        cols = slice(h * HEAD, (h + 1) * HEAD)
        query = qn_ref[:, cols]
        grad = grad_ref[:, cols]
        inner = (grad.astype(f32) * out_ref[:, cols].astype(f32)).T
        inner = jnp.sum(inner, axis=0, keepdims=True)
        lse = lse_ref[h : h + 1]
        for c in range(CHUNKS):
            rows = slice(c * BLOCK, (c + 1) * BLOCK)
            if c < PROMPT_CHUNKS:
                value = kv_ref[rows, HEAD:]
            else:
                value = v_ref[(c - PROMPT_CHUNKS) * BLOCK : (c - PROMPT_CHUNKS + 1) * BLOCK]
            scores = masked(nt(keys_ref[rows], query) * SCALE, c, length)
            weights = jnp.exp(scores - lse)
            prob_grad = nt(value, grad)
            score_grad = (weights * (prob_grad - inner) * SCALE).astype(bf16)
            ds_ref[rows] = score_grad
            key_term = nn(score_grad, query)
            value_term = nn(weights.astype(bf16), grad)
            if h == 0:
                dk_ref[rows] = key_term
                dv_ref[rows] = value_term
            else:
                dk_ref[rows] += key_term
                dv_ref[rows] += value_term
        grad_qn = nn(keys_t_ref[...], ds_ref[...]).T
        normed = q_ref[:, cols].astype(f32) * query_factor
        u = grad_qn * qg_ref[:, cols]
        u_ref[:, cols] = u
        query_mix = query_mix + jnp.sum(u * normed, axis=1, keepdims=True)
        gain_rows.append(jnp.sum(grad_qn * normed, axis=0, keepdims=True))
    terms_ref[:, :HEAD] = dk_ref[:PROMPT]
    terms_ref[:, HEAD:] = dv_ref[:PROMPT]
    gv_ref[...] = dv_ref[PROMPT:].astype(bf16)
    grad_kn = dk_ref[PROMPT:]
    normed_key = k_ref[...].astype(f32) * key_factor
    w = grad_kn * kg_ref[...]
    w_ref[...] = w
    key_mix = jnp.sum(w * normed_key, axis=1, keepdims=True)
    gain_rows.append(jnp.sum(grad_kn * normed_key, axis=0, keepdims=True))
    gains = jnp.concatenate(
        [jnp.concatenate(gain_rows[i : i + 2], axis=1) for i in range(0, GROUP + 1, 2)], axis=0
    )
    gain_ref[...] = jnp.concatenate(
        [gains, jnp.zeros((8 - GAIN_ROWS, 2 * HEAD), f32)], axis=0
    )
    tile = columns_to_tile([query_mix[:BLOCK], query_mix[BLOCK:], key_mix[:BLOCK], key_mix[BLOCK:]])
    mix_ref[...] = tile


def final_kernel(q_ref, k_ref, sums_ref, u_ref, w_ref, *refs):
    *mix_refs, gq_ref, gk_ref = refs
    query_factor, key_factor = factors(sums_ref)
    total = mix_refs[0][...]
    for mix_ref in mix_refs[1:]:
        total = total + mix_ref[...]
    query_mix, key_mix = tile_to_columns(total)
    normed = q_ref[...].astype(f32) * query_factor
    gq_ref[...] = (
        query_factor * (u_ref[...] - normed * (query_mix / (HEADS * HEAD)))
    ).astype(bf16)
    normed_key = k_ref[...].astype(f32) * key_factor
    gk_ref[...] = (
        key_factor * (w_ref[...] - normed_key * (key_mix / (KV_HEADS * HEAD)))
    ).astype(bf16)


def call(kernel, outs, specs, scratch, flops, *args):
    return pl.pallas_call(
        kernel,
        out_shape=[jax.ShapeDtypeStruct(s, d) for s, d in outs],
        in_specs=specs,
        out_specs=[VMEM] * len(outs),
        scratch_shapes=[pltpu.VMEM(s, d) for s, d in scratch],
        compiler_params=PARAMS,
        cost_estimate=pl.CostEstimate(flops=flops, bytes_accessed=0, transcendentals=0),
    )(*args)


def after(array, *others):
    return lax.optimization_barrier((array,) + others)[0]


def swap(array, even, odd):
    pairs = [(i, i ^ (odd if i % 2 else even)) for i in range(N_TRAINER)]
    return lax.ppermute(array, TRAINER, pairs)


class Route:
    def __init__(self, me, source):
        self.me, self.source = me, source
        self.core = me & 1
        self.first = jnp.where(self.core == 0, 8, 4)
        self.last = 12 - self.first

    def pair(self, blocks):
        mine = lax.dynamic_index_in_dim(blocks, self.core, 0, keepdims=False)
        other = lax.dynamic_index_in_dim(blocks, 1 - self.core, 0, keepdims=False)
        return jnp.stack([mine, swap(other, 1, 1)])

    def four(self, pair, *earlier):
        return jnp.concatenate([pair, after(swap(pair, 8, 4), *earlier)], axis=0)

    def eight(self, four):
        return four, swap(four, 2, 2)

    def pick(self, eight, source):
        offset = source ^ self.me
        slot = bit(offset, 1) + 2 * bit(offset, self.first)
        near, far = (lax.dynamic_index_in_dim(four, slot, 0, keepdims=False) for four in eight)
        return jnp.where((offset & 2) != 0, far, near)

    def wanted(self, eight):
        there = self.me ^ self.last
        return jnp.stack([self.pick(eight, self.source(there ^ i, self.core)) for i in range(2)])

    def found(self, eight, wanted, *earlier):
        came = after(swap(wanted, 4, 8), *earlier)
        found = []
        for i in range(2):
            source = self.source(self.me ^ i, self.core)
            far = ((source ^ self.me) & self.last) != 0
            found.append(jnp.where(far, came[i], self.pick(eight, source)))
        return found

    def passed(self, found):
        return swap(found, 1, 1)


def bit(number, mask):
    return jnp.where((number & mask) != 0, 1, 0)


def on_device(
    queries,
    resp_keys,
    resp_values,
    prompt_keys,
    prompt_values,
    q_gain,
    k_gain,
    lengths,
    block_rank,
    out_grad,
):
    me = lax.axis_index(TRAINER)
    core = me & 1
    table = block_rank[0]
    ranks = jnp.arange(N_TRAINER, dtype=jnp.int32)

    def home_source(dest, b):
        return lax.dynamic_index_in_dim(table[:, b], dest, 0, keepdims=False)

    def balanced_source(dest, b):
        return jnp.sum(jnp.where(table[:, b] == dest, ranks, 0))

    query, key, value = queries[0, 0], resp_keys[0, 0], resp_values[0, 0]
    q_row, k_row = q_gain[None], k_gain[None]

    sums, pairs = call(
        stats_kernel,
        [((N_TENSOR, 8, BLOCK), f32), ((N_TRAINER, PROMPT // N_TRAINER, 2 * HEAD), bf16)],
        [VMEM] * 4,
        [],
        0,
        query,
        key,
        prompt_keys[0],
        prompt_values[0],
    )
    to_home = Route(me, home_source)
    grad_pair, sums, pairs = lax.optimization_barrier(
        (to_home.pair(out_grad.reshape(BLOCKS, BLOCK, WIDTH)), sums, pairs)
    )
    sums = lax.all_to_all(sums, "tensor", 0, 0, tiled=True)
    grad_four = to_home.four(grad_pair, sums)
    grad_four, pairs = lax.optimization_barrier((grad_four, pairs))
    grad_eight = to_home.eight(grad_four)
    pairs = lax.all_to_all(pairs, TRAINER, 0, 0, tiled=True).reshape(PROMPT, 2 * HEAD)
    grad_wanted = to_home.wanted(grad_eight)
    pairs = after(pairs, grad_wanted)
    grad_found = to_home.found(grad_eight, grad_wanted)
    info = jnp.stack([lengths[0, 0], core])
    shared = (query, key, value, pairs, sums, q_row, k_row)
    query_n, key_list, lse, home_out = call(
        forward_kernel,
        [((RESP, WIDTH), bf16), ((KEYS, HEAD), bf16), ((8, RESP), f32), ((RESP, WIDTH), bf16)],
        [SMEM] + [VMEM] * 7,
        [((HEAD, KEYS), bf16), ((KEYS, RESP), f32), ((KEYS, RESP), bf16)],
        0,
        info,
        *shared,
    )

    to_ranks = Route(me, balanced_source)
    out_pair = to_ranks.pair(home_out.reshape(BLOCKS, BLOCK, WIDTH))
    grad_found[1], out_pair = lax.optimization_barrier((grad_found[1], out_pair))
    out_four = to_ranks.four(out_pair)
    grad_own = grad_found[0]
    grad_passed = to_home.passed(grad_found[1])

    u, w, grad_values, terms, mix, gains = call(
        backward_kernel,
        [
            ((RESP, WIDTH), f32),
            ((RESP, HEAD), f32),
            ((RESP, HEAD), bf16),
            ((PROMPT, 2 * HEAD), f32),
            ((8, BLOCK), f32),
            ((8, 2 * HEAD), f32),
        ],
        [SMEM] + [VMEM] * 13,
        [
            ((HEAD, KEYS), bf16),
            ((RESP, WIDTH), bf16),
            ((KEYS, RESP), bf16),
            ((KEYS, HEAD), f32),
            ((KEYS, HEAD), f32),
        ],
        0,
        info,
        *shared,
        query_n,
        key_list,
        lse,
        home_out,
        grad_own,
        grad_passed,
    )
    out_four, gains, terms = lax.optimization_barrier((out_four, gains, terms))
    out_eight = to_ranks.eight(out_four)
    turns = [[(i, (i + k) % N_TENSOR) for i in range(N_TENSOR)] for k in range(1, N_TENSOR)]
    mix = [mix] + [lax.ppermute(mix, "tensor", turn) for turn in turns]
    owned = PROMPT // N_TRAINER
    terms = jnp.concatenate(
        [
            terms.reshape(N_TRAINER, owned, 2 * HEAD),
            jnp.broadcast_to(gains[None], (N_TRAINER,) + gains.shape),
        ],
        axis=1,
    ).reshape(N_TRAINER // 2, 2, owned + gains.shape[0], 2 * HEAD)
    near, far = (
        lax.dynamic_index_in_dim(terms, i, 1, keepdims=False) for i in (core, 1 - core)
    )
    terms = (near + swap(far.astype(bf16), 1, 1).astype(f32)).astype(bf16)
    terms = lax.all_to_all(terms, "zlo", 0, 0, tiled=True)
    terms = jnp.sum(terms.astype(f32), axis=0)
    gains = terms[owned : owned + GAIN_ROWS]
    terms = terms[:owned].astype(bf16)
    out_wanted = to_ranks.wanted(out_eight)
    gains = after(gains, out_wanted)
    gains = lax.all_to_all(
        jnp.broadcast_to(gains[None], (lax.axis_size(PROMPTS),) + gains.shape),
        PROMPTS,
        0,
        0,
        tiled=True,
    )
    gains = jnp.sum(gains, axis=0).reshape(-1)
    out_found = to_ranks.found(out_eight, out_wanted)

    out_own, out_passed = out_found[0], to_ranks.passed(after(out_found[1], gains))
    attn_out = jnp.where(
        core == 0,
        jnp.concatenate([out_own, out_passed], axis=0),
        jnp.concatenate([out_passed, out_own], axis=0),
    )
    grad_queries, grad_keys = call(
        final_kernel,
        [((RESP, WIDTH), bf16), ((RESP, HEAD), bf16)],
        [VMEM] * (5 + N_TENSOR),
        [],
        0,
        query,
        key,
        sums,
        u,
        w,
        *mix,
    )
    return (
        attn_out[None, None],
        grad_queries[None, None],
        grad_keys[None, None],
        grad_values[None, None],
        terms[None, :, :HEAD],
        terms[None, :, HEAD:],
        gains[:WIDTH],
        gains[WIDTH : WIDTH + HEAD],
    )


def solution(mesh):
    n_zhi = 2 if mesh.shape["prompt"] % 2 == 0 else 1
    shape = (mesh.shape["prompt"] // n_zhi, n_zhi, N_TRAINER // 2, 2, N_TENSOR)
    fine = jax.sharding.Mesh(mesh.devices.reshape(shape), PROMPTS + TRAINER + ("tensor",))
    rows = P(PROMPTS, TRAINER, None, "tensor")
    tokens = P(PROMPTS, TRAINER, "tensor")
    return jax.shard_map(
        on_device,
        mesh=fine,
        in_specs=(
            rows,
            rows,
            rows,
            tokens,
            tokens,
            P("tensor"),
            P("tensor"),
            P(PROMPTS, TRAINER),
            P(PROMPTS, None, None),
            rows,
        ),
        out_specs=(rows, rows, rows, rows, tokens, tokens, P("tensor"), P("tensor")),
        check_vma=False,
    )
```

```python
import jax
import jax.numpy as jnp
from jax import lax
from jax.experimental import pallas as pl
from jax.experimental.pallas import tpu as pltpu
from jax.sharding import PartitionSpec as P

HEAD = 128
HEADS = 20
KV_HEADS = 4
GROUP = HEADS // KV_HEADS
BLOCK = 128
BLOCKS = 2
RESP = BLOCK * BLOCKS
PROMPT = 512
KEYS = PROMPT + RESP
CHUNKS = KEYS // BLOCK
PROMPT_CHUNKS = PROMPT // BLOCK
N_TRAINER = 16
N_TENSOR = 4
PROMPTS = ("x", "zhi")
TRAINER = ("zlo", "core")
WIDTH = GROUP * HEAD
GAIN_ROWS = (GROUP + 1) // 2
SCALE = HEAD ** (-0.5)

epsilon = 1e-06
f32 = jnp.float32
bf16 = jnp.bfloat16

PARAMS = pltpu.CompilerParams(vmem_limit_bytes=24 * 1024 * 1024)
VMEM = pl.BlockSpec(memory_space=pltpu.VMEM)
SMEM = pl.BlockSpec(memory_space=pltpu.SMEM)


def nt(left, right):
    return lax.dot_general(left, right, (((1,), (1,)), ((), ())), preferred_element_type=f32)


def nn(left, right):
    return jnp.dot(left, right, preferred_element_type=f32)


def columns_to_tile(columns):
    wide = [jnp.broadcast_to(c, (BLOCK, BLOCK)).T[:1] for c in columns]
    wide.append(jnp.zeros((8 - len(columns), BLOCK), f32))
    return jnp.concatenate(wide, axis=0)


def tile_to_columns(tile):
    turned = jnp.concatenate([tile] * (BLOCK // 8), axis=0).T
    first = jnp.concatenate([turned[:, 0:1], turned[:, 1:2]], axis=0)
    second = jnp.concatenate([turned[:, 2:3], turned[:, 3:4]], axis=0)
    return first, second


def factors(sums_ref):
    total = sums_ref[0]
    for i in range(1, N_TENSOR):
        total = total + sums_ref[i]
    query_sums, key_sums = tile_to_columns(total)
    query_factor = lax.rsqrt(query_sums / (HEADS * HEAD) + epsilon)
    key_factor = lax.rsqrt(key_sums / (KV_HEADS * HEAD) + epsilon)
    return query_factor, key_factor


def stats_kernel(q_ref, k_ref, pk_ref, pv_ref, sums_ref, kv_ref):
    raw_query = q_ref[...].astype(f32)
    raw_key = k_ref[...].astype(f32)
    query_sums = jnp.sum(raw_query * raw_query, axis=1, keepdims=True)
    key_sums = jnp.sum(raw_key * raw_key, axis=1, keepdims=True)
    tile = columns_to_tile(
        [query_sums[:BLOCK], query_sums[BLOCK:], key_sums[:BLOCK], key_sums[BLOCK:]]
    )
    for i in range(N_TENSOR):
        sums_ref[i] = tile
    pair = jnp.concatenate([pk_ref[...], pv_ref[...]], axis=1)
    for i in range(N_TRAINER):
        kv_ref[i] = pair


def masked(scores, chunk, length):
    if chunk < PROMPT_CHUNKS:
        return scores
    key_pos = lax.broadcasted_iota(jnp.int32, scores.shape, 0) + (chunk - PROMPT_CHUNKS) * BLOCK
    query_pos = lax.broadcasted_iota(jnp.int32, scores.shape, 1)
    return jnp.where((key_pos <= query_pos) & (key_pos < length), scores, -1e30)


def live_column(length):
    rows = lax.broadcasted_iota(jnp.int32, (RESP, 1), 0)
    return (rows < length).astype(f32)


def forward_kernel(
    info_ref, q_ref, k_ref, v_ref, kv_ref, sums_ref, qg_ref, kg_ref,
    qn_ref, keys_ref, lse_ref, out_ref,
    values_t_ref, s_ref, p_ref,
):
    length = info_ref[0]
    query_factor, key_factor = factors(sums_ref)
    qn_ref[...] = (q_ref[...].astype(f32) * query_factor * qg_ref[...]).astype(bf16)
    keys_ref[:PROMPT] = kv_ref[:, :HEAD]
    keys_ref[PROMPT:] = (k_ref[...].astype(f32) * key_factor * kg_ref[...]).astype(bf16)
    values_t_ref[:, :PROMPT] = kv_ref[:, HEAD:].astype(f32).T.astype(bf16)
    values_t_ref[:, PROMPT:] = v_ref[...].astype(f32).T.astype(bf16)
    live = live_column(length)
    for h in range(GROUP):
        cols = slice(h * HEAD, (h + 1) * HEAD)
        query = qn_ref[:, cols]
        top = None
        for c in range(CHUNKS):
            rows = slice(c * BLOCK, (c + 1) * BLOCK)
            scores = masked(nt(keys_ref[rows], query) * SCALE, c, length)
            s_ref[rows] = scores
            most = jnp.max(scores, axis=0, keepdims=True)
            top = most if top is None else jnp.maximum(top, most)
        total = jnp.zeros_like(top)
        for c in range(CHUNKS):
            rows = slice(c * BLOCK, (c + 1) * BLOCK)
            grown = jnp.exp(s_ref[rows] - top)
            s_ref[rows] = grown
            total = total + jnp.sum(grown, axis=0, keepdims=True)
        share = 1.0 / total
        for c in range(CHUNKS):
            rows = slice(c * BLOCK, (c + 1) * BLOCK)
            p_ref[rows] = (s_ref[rows] * share).astype(bf16)
        lse_ref[h : h + 1] = top + jnp.log(total)
        attended = nn(values_t_ref[...], p_ref[...]).T
        out_ref[:, cols] = (attended * live).astype(bf16)
    lse_ref[GROUP:] = jnp.zeros((8 - GROUP, RESP), f32)


def backward_kernel(
    info_ref, q_ref, k_ref, v_ref, kv_ref, sums_ref, qg_ref, kg_ref,
    qn_ref, keys_ref, lse_ref, out_ref, own_ref, passed_ref,
    u_ref, w_ref, gv_ref, terms_ref, mix_ref, gain_ref,
    keys_t_ref, grad_ref, ds_ref, dk_ref, dv_ref,
):
    length = info_ref[0]
    query_factor, key_factor = factors(sums_ref)
    keys_t_ref[...] = keys_ref[...].astype(f32).T.astype(bf16)
    live = live_column(length).astype(bf16)
    swapped = info_ref[1] != 0
    first = jnp.where(swapped, passed_ref[...], own_ref[...])
    second = jnp.where(swapped, own_ref[...], passed_ref[...])
    grad_ref[:BLOCK] = first * live[:BLOCK]
    grad_ref[BLOCK:] = second * live[BLOCK:]
    query_mix = jnp.zeros((RESP, 1), f32)
    gain_rows = []
    for h in range(GROUP):
        cols = slice(h * HEAD, (h + 1) * HEAD)
        query = qn_ref[:, cols]
        grad = grad_ref[:, cols]
        inner = (grad.astype(f32) * out_ref[:, cols].astype(f32)).T
        inner = jnp.sum(inner, axis=0, keepdims=True)
        lse = lse_ref[h : h + 1]
        for c in range(CHUNKS):
            rows = slice(c * BLOCK, (c + 1) * BLOCK)
            if c < PROMPT_CHUNKS:
                value = kv_ref[rows, HEAD:]
            else:
                value = v_ref[(c - PROMPT_CHUNKS) * BLOCK : (c - PROMPT_CHUNKS + 1) * BLOCK]
            scores = masked(nt(keys_ref[rows], query) * SCALE, c, length)
            weights = jnp.exp(scores - lse)
            prob_grad = nt(value, grad)
            score_grad = (weights * (prob_grad - inner) * SCALE).astype(bf16)
            ds_ref[rows] = score_grad
            key_term = nn(score_grad, query)
            value_term = nn(weights.astype(bf16), grad)
            if h == 0:
                dk_ref[rows] = key_term
                dv_ref[rows] = value_term
            else:
                dk_ref[rows] += key_term
                dv_ref[rows] += value_term
        grad_qn = nn(keys_t_ref[...], ds_ref[...]).T
        normed = q_ref[:, cols].astype(f32) * query_factor
        u = grad_qn * qg_ref[:, cols]
        u_ref[:, cols] = u
        query_mix = query_mix + jnp.sum(u * normed, axis=1, keepdims=True)
        gain_rows.append(jnp.sum(grad_qn * normed, axis=0, keepdims=True))
    terms_ref[:, :HEAD] = dk_ref[:PROMPT]
    terms_ref[:, HEAD:] = dv_ref[:PROMPT]
    gv_ref[...] = dv_ref[PROMPT:].astype(bf16)
    grad_kn = dk_ref[PROMPT:]
    normed_key = k_ref[...].astype(f32) * key_factor
    w = grad_kn * kg_ref[...]
    w_ref[...] = w
    key_mix = jnp.sum(w * normed_key, axis=1, keepdims=True)
    gain_rows.append(jnp.sum(grad_kn * normed_key, axis=0, keepdims=True))
    gains = jnp.concatenate(
        [jnp.concatenate(gain_rows[i : i + 2], axis=1) for i in range(0, GROUP + 1, 2)], axis=0
    )
    gain_ref[...] = jnp.concatenate(
        [gains, jnp.zeros((8 - GAIN_ROWS, 2 * HEAD), f32)], axis=0
    )
    tile = columns_to_tile([query_mix[:BLOCK], query_mix[BLOCK:], key_mix[:BLOCK], key_mix[BLOCK:]])
    for i in range(N_TENSOR):
        mix_ref[i] = tile


def final_kernel(q_ref, k_ref, sums_ref, u_ref, w_ref, mix_ref, gq_ref, gk_ref):
    query_factor, key_factor = factors(sums_ref)
    total = mix_ref[0]
    for i in range(1, N_TENSOR):
        total = total + mix_ref[i]
    query_mix, key_mix = tile_to_columns(total)
    normed = q_ref[...].astype(f32) * query_factor
    gq_ref[...] = (
        query_factor * (u_ref[...] - normed * (query_mix / (HEADS * HEAD)))
    ).astype(bf16)
    normed_key = k_ref[...].astype(f32) * key_factor
    gk_ref[...] = (
        key_factor * (w_ref[...] - normed_key * (key_mix / (KV_HEADS * HEAD)))
    ).astype(bf16)


def call(kernel, outs, specs, scratch, flops, *args):
    return pl.pallas_call(
        kernel,
        out_shape=[jax.ShapeDtypeStruct(s, d) for s, d in outs],
        in_specs=specs,
        out_specs=[VMEM] * len(outs),
        scratch_shapes=[pltpu.VMEM(s, d) for s, d in scratch],
        compiler_params=PARAMS,
        cost_estimate=pl.CostEstimate(flops=flops, bytes_accessed=0, transcendentals=0),
    )(*args)


def after(array, *others):
    return lax.optimization_barrier((array,) + others)[0]


def swap(array, even, odd):
    pairs = [(i, i ^ (odd if i % 2 else even)) for i in range(N_TRAINER)]
    return lax.ppermute(array, TRAINER, pairs)


class Route:
    def __init__(self, me, source):
        self.me, self.source = me, source
        self.core = me & 1
        self.first = jnp.where(self.core == 0, 8, 4)
        self.last = 12 - self.first

    def pair(self, blocks):
        mine = lax.dynamic_index_in_dim(blocks, self.core, 0, keepdims=False)
        other = lax.dynamic_index_in_dim(blocks, 1 - self.core, 0, keepdims=False)
        return jnp.stack([mine, swap(other, 1, 1)])

    def four(self, pair, *earlier):
        return jnp.concatenate([pair, after(swap(pair, 8, 4), *earlier)], axis=0)

    def eight(self, four):
        return four, swap(four, 2, 2)

    def pick(self, eight, source):
        offset = source ^ self.me
        slot = bit(offset, 1) + 2 * bit(offset, self.first)
        near, far = (lax.dynamic_index_in_dim(four, slot, 0, keepdims=False) for four in eight)
        return jnp.where((offset & 2) != 0, far, near)

    def wanted(self, eight):
        there = self.me ^ self.last
        return jnp.stack([self.pick(eight, self.source(there ^ i, self.core)) for i in range(2)])

    def found(self, eight, wanted, *earlier):
        came = after(swap(wanted, 4, 8), *earlier)
        found = []
        for i in range(2):
            source = self.source(self.me ^ i, self.core)
            far = ((source ^ self.me) & self.last) != 0
            found.append(jnp.where(far, came[i], self.pick(eight, source)))
        return found

    def passed(self, found):
        return swap(found, 1, 1)


def bit(number, mask):
    return jnp.where((number & mask) != 0, 1, 0)


def on_device(
    queries,
    resp_keys,
    resp_values,
    prompt_keys,
    prompt_values,
    q_gain,
    k_gain,
    lengths,
    block_rank,
    out_grad,
):
    me = lax.axis_index(TRAINER)
    core = me & 1
    table = block_rank[0]
    ranks = jnp.arange(N_TRAINER, dtype=jnp.int32)

    def home_source(dest, b):
        return lax.dynamic_index_in_dim(table[:, b], dest, 0, keepdims=False)

    def balanced_source(dest, b):
        return jnp.sum(jnp.where(table[:, b] == dest, ranks, 0))

    query, key, value = queries[0, 0], resp_keys[0, 0], resp_values[0, 0]
    q_row, k_row = q_gain[None], k_gain[None]

    sums, pairs = call(
        stats_kernel,
        [((N_TENSOR, 8, BLOCK), f32), ((N_TRAINER, PROMPT // N_TRAINER, 2 * HEAD), bf16)],
        [VMEM] * 4,
        [],
        0,
        query,
        key,
        prompt_keys[0],
        prompt_values[0],
    )
    to_home = Route(me, home_source)
    grad_pair, sums, pairs = lax.optimization_barrier(
        (to_home.pair(out_grad.reshape(BLOCKS, BLOCK, WIDTH)), sums, pairs)
    )
    sums = lax.all_to_all(sums, "tensor", 0, 0, tiled=True)
    grad_four = to_home.four(grad_pair, sums)
    grad_four, pairs = lax.optimization_barrier((grad_four, pairs))
    grad_eight = to_home.eight(grad_four)
    pairs = lax.all_to_all(pairs, TRAINER, 0, 0, tiled=True).reshape(PROMPT, 2 * HEAD)
    grad_wanted = to_home.wanted(grad_eight)
    pairs = after(pairs, grad_wanted)
    grad_found = to_home.found(grad_eight, grad_wanted)
    info = jnp.stack([lengths[0, 0], core])
    shared = (query, key, value, pairs, sums, q_row, k_row)
    query_n, key_list, lse, home_out = call(
        forward_kernel,
        [((RESP, WIDTH), bf16), ((KEYS, HEAD), bf16), ((8, RESP), f32), ((RESP, WIDTH), bf16)],
        [SMEM] + [VMEM] * 7,
        [((HEAD, KEYS), bf16), ((KEYS, RESP), f32), ((KEYS, RESP), bf16)],
        0,
        info,
        *shared,
    )

    to_ranks = Route(me, balanced_source)
    out_pair = to_ranks.pair(home_out.reshape(BLOCKS, BLOCK, WIDTH))
    grad_found[1], out_pair = lax.optimization_barrier((grad_found[1], out_pair))
    out_four = to_ranks.four(out_pair)
    grad_own = grad_found[0]
    grad_passed = to_home.passed(grad_found[1])

    u, w, grad_values, terms, mix, gains = call(
        backward_kernel,
        [
            ((RESP, WIDTH), f32),
            ((RESP, HEAD), f32),
            ((RESP, HEAD), bf16),
            ((PROMPT, 2 * HEAD), f32),
            ((N_TENSOR, 8, BLOCK), f32),
            ((8, 2 * HEAD), f32),
        ],
        [SMEM] + [VMEM] * 13,
        [
            ((HEAD, KEYS), bf16),
            ((RESP, WIDTH), bf16),
            ((KEYS, RESP), bf16),
            ((KEYS, HEAD), f32),
            ((KEYS, HEAD), f32),
        ],
        0,
        info,
        *shared,
        query_n,
        key_list,
        lse,
        home_out,
        grad_own,
        grad_passed,
    )
    out_four, gains, terms = lax.optimization_barrier((out_four, gains, terms))
    out_eight = to_ranks.eight(out_four)
    owned = PROMPT // N_TRAINER
    terms = jnp.concatenate(
        [
            terms.reshape(N_TRAINER, owned, 2 * HEAD),
            jnp.broadcast_to(gains[None], (N_TRAINER,) + gains.shape),
        ],
        axis=1,
    ).reshape(N_TRAINER // 2, 2, owned + gains.shape[0], 2 * HEAD)
    near, far = (
        lax.dynamic_index_in_dim(terms, i, 1, keepdims=False) for i in (core, 1 - core)
    )
    terms = (near + swap(far.astype(bf16), 1, 1).astype(f32)).astype(bf16)
    mix = lax.all_to_all(mix, "tensor", 0, 0, tiled=True)
    terms = lax.all_to_all(after(terms, mix), "zlo", 0, 0, tiled=True)
    terms = jnp.sum(terms.astype(f32), axis=0)
    gains = terms[owned : owned + GAIN_ROWS]
    terms = terms[:owned].astype(bf16)
    out_wanted = to_ranks.wanted(out_eight)
    gains = after(gains, out_wanted)
    gains = lax.all_to_all(
        jnp.broadcast_to(gains[None], (lax.axis_size(PROMPTS),) + gains.shape),
        PROMPTS,
        0,
        0,
        tiled=True,
    )
    gains = jnp.sum(gains, axis=0).reshape(-1)
    out_found = to_ranks.found(out_eight, out_wanted)

    out_own, out_passed = out_found[0], to_ranks.passed(after(out_found[1], gains))
    attn_out = jnp.where(
        core == 0,
        jnp.concatenate([out_own, out_passed], axis=0),
        jnp.concatenate([out_passed, out_own], axis=0),
    )
    grad_queries, grad_keys = call(
        final_kernel,
        [((RESP, WIDTH), bf16), ((RESP, HEAD), bf16)],
        [VMEM] * 6,
        [],
        0,
        query,
        key,
        sums,
        u,
        w,
        mix,
    )
    return (
        attn_out[None, None],
        grad_queries[None, None],
        grad_keys[None, None],
        grad_values[None, None],
        terms[None, :, :HEAD],
        terms[None, :, HEAD:],
        gains[:WIDTH],
        gains[WIDTH : WIDTH + HEAD],
    )


def solution(mesh):
    n_zhi = 2 if mesh.shape["prompt"] % 2 == 0 else 1
    shape = (mesh.shape["prompt"] // n_zhi, n_zhi, N_TRAINER // 2, 2, N_TENSOR)
    fine = jax.sharding.Mesh(mesh.devices.reshape(shape), PROMPTS + TRAINER + ("tensor",))
    rows = P(PROMPTS, TRAINER, None, "tensor")
    tokens = P(PROMPTS, TRAINER, "tensor")
    return jax.shard_map(
        on_device,
        mesh=fine,
        in_specs=(
            rows,
            rows,
            rows,
            tokens,
            tokens,
            P("tensor"),
            P("tensor"),
            P(PROMPTS, TRAINER),
            P(PROMPTS, None, None),
            rows,
        ),
        out_specs=(rows, rows, rows, rows, tokens, tokens, P("tensor"), P("tensor")),
        check_vma=False,
    )
```

```python
import jax
import jax.numpy as jnp
from jax import lax
from jax.experimental import pallas as pl
from jax.experimental.pallas import tpu as pltpu
from jax.sharding import PartitionSpec as P

HEAD = 128
HEADS = 20
KV_HEADS = 4
GROUP = HEADS // KV_HEADS
BLOCK = 128
BLOCKS = 2
RESP = BLOCK * BLOCKS
PROMPT = 512
KEYS = PROMPT + RESP
CHUNKS = KEYS // BLOCK
PROMPT_CHUNKS = PROMPT // BLOCK
N_TRAINER = 16
N_TENSOR = 4
PROMPTS = ("x", "zhi")
TRAINER = ("zlo", "core")
WIDTH = GROUP * HEAD
GAIN_ROWS = (GROUP + 1) // 2
SCALE = HEAD ** (-0.5)

epsilon = 1e-06
f32 = jnp.float32
bf16 = jnp.bfloat16

PARAMS = pltpu.CompilerParams(vmem_limit_bytes=24 * 1024 * 1024)
VMEM = pl.BlockSpec(memory_space=pltpu.VMEM)
SMEM = pl.BlockSpec(memory_space=pltpu.SMEM)


def nt(left, right):
    return lax.dot_general(left, right, (((1,), (1,)), ((), ())), preferred_element_type=f32)


def nn(left, right):
    return jnp.dot(left, right, preferred_element_type=f32)


def columns_to_tile(columns):
    wide = [jnp.broadcast_to(c, (BLOCK, BLOCK)).T[:1] for c in columns]
    wide.append(jnp.zeros((8 - len(columns), BLOCK), f32))
    return jnp.concatenate(wide, axis=0)


def tile_to_columns(tile):
    turned = jnp.concatenate([tile] * (BLOCK // 8), axis=0).T
    first = jnp.concatenate([turned[:, 0:1], turned[:, 1:2]], axis=0)
    second = jnp.concatenate([turned[:, 2:3], turned[:, 3:4]], axis=0)
    return first, second


def factors(sums_ref):
    total = sums_ref[0]
    for i in range(1, N_TENSOR):
        total = total + sums_ref[i]
    query_sums, key_sums = tile_to_columns(total)
    query_factor = lax.rsqrt(query_sums / (HEADS * HEAD) + epsilon)
    key_factor = lax.rsqrt(key_sums / (KV_HEADS * HEAD) + epsilon)
    return query_factor, key_factor


def stats_kernel(q_ref, k_ref, pk_ref, pv_ref, sums_ref, kv_ref):
    raw_query = q_ref[...].astype(f32)
    raw_key = k_ref[...].astype(f32)
    query_sums = jnp.sum(raw_query * raw_query, axis=1, keepdims=True)
    key_sums = jnp.sum(raw_key * raw_key, axis=1, keepdims=True)
    tile = columns_to_tile(
        [query_sums[:BLOCK], query_sums[BLOCK:], key_sums[:BLOCK], key_sums[BLOCK:]]
    )
    for i in range(N_TENSOR):
        sums_ref[i] = tile
    pair = jnp.concatenate([pk_ref[...], pv_ref[...]], axis=1)
    for i in range(N_TRAINER):
        kv_ref[i] = pair


def masked(scores, chunk, length):
    if chunk < PROMPT_CHUNKS:
        return scores
    key_pos = lax.broadcasted_iota(jnp.int32, scores.shape, 0) + (chunk - PROMPT_CHUNKS) * BLOCK
    query_pos = lax.broadcasted_iota(jnp.int32, scores.shape, 1)
    return jnp.where((key_pos <= query_pos) & (key_pos < length), scores, -1e30)


def live_column(length):
    rows = lax.broadcasted_iota(jnp.int32, (RESP, 1), 0)
    return (rows < length).astype(f32)


def forward_kernel(
    info_ref, q_ref, k_ref, v_ref, near_ref, far_ref, sums_ref, qg_ref, kg_ref,
    qn_ref, keys_ref, lse_ref, out_ref,
    values_t_ref, s_ref, p_ref,
):
    length = info_ref[0]
    query_factor, key_factor = factors(sums_ref)
    qn_ref[...] = (q_ref[...].astype(f32) * query_factor * qg_ref[...]).astype(bf16)
    keys_ref[:RESP] = near_ref[:, :HEAD]
    keys_ref[RESP:PROMPT] = far_ref[:, :HEAD]
    keys_ref[PROMPT:] = (k_ref[...].astype(f32) * key_factor * kg_ref[...]).astype(bf16)
    values_t_ref[:, :RESP] = near_ref[:, HEAD:].astype(f32).T.astype(bf16)
    values_t_ref[:, RESP:PROMPT] = far_ref[:, HEAD:].astype(f32).T.astype(bf16)
    values_t_ref[:, PROMPT:] = v_ref[...].astype(f32).T.astype(bf16)
    live = live_column(length)
    for h in range(GROUP):
        cols = slice(h * HEAD, (h + 1) * HEAD)
        query = qn_ref[:, cols]
        top = None
        for c in range(CHUNKS):
            rows = slice(c * BLOCK, (c + 1) * BLOCK)
            scores = masked(nt(keys_ref[rows], query) * SCALE, c, length)
            s_ref[rows] = scores
            most = jnp.max(scores, axis=0, keepdims=True)
            top = most if top is None else jnp.maximum(top, most)
        total = jnp.zeros_like(top)
        for c in range(CHUNKS):
            rows = slice(c * BLOCK, (c + 1) * BLOCK)
            grown = jnp.exp(s_ref[rows] - top)
            s_ref[rows] = grown
            total = total + jnp.sum(grown, axis=0, keepdims=True)
        share = 1.0 / total
        for c in range(CHUNKS):
            rows = slice(c * BLOCK, (c + 1) * BLOCK)
            p_ref[rows] = (s_ref[rows] * share).astype(bf16)
        lse_ref[h : h + 1] = top + jnp.log(total)
        attended = nn(values_t_ref[...], p_ref[...]).T
        out_ref[:, cols] = (attended * live).astype(bf16)
    lse_ref[GROUP:] = jnp.zeros((8 - GROUP, RESP), f32)


def backward_kernel(
    info_ref, q_ref, k_ref, v_ref, near_ref, far_ref, sums_ref, qg_ref, kg_ref,
    qn_ref, keys_ref, lse_ref, out_ref, own_ref, passed_ref,
    u_ref, w_ref, gv_ref, near_terms_ref, far_terms_ref, small_ref,
    keys_t_ref, grad_ref, ds_ref, dk_ref, dv_ref,
):
    length = info_ref[0]
    query_factor, key_factor = factors(sums_ref)
    keys_t_ref[...] = keys_ref[...].astype(f32).T.astype(bf16)
    live = live_column(length).astype(bf16)
    swapped = info_ref[1] != 0
    first = jnp.where(swapped, passed_ref[...], own_ref[...])
    second = jnp.where(swapped, own_ref[...], passed_ref[...])
    grad_ref[:BLOCK] = first * live[:BLOCK]
    grad_ref[BLOCK:] = second * live[BLOCK:]
    query_mix = jnp.zeros((RESP, 1), f32)
    gain_rows = []
    for h in range(GROUP):
        cols = slice(h * HEAD, (h + 1) * HEAD)
        query = qn_ref[:, cols]
        grad = grad_ref[:, cols]
        inner = (grad.astype(f32) * out_ref[:, cols].astype(f32)).T
        inner = jnp.sum(inner, axis=0, keepdims=True)
        lse = lse_ref[h : h + 1]
        for c in range(CHUNKS):
            rows = slice(c * BLOCK, (c + 1) * BLOCK)
            part = slice(c % 2 * BLOCK, (c % 2 + 1) * BLOCK)
            value = (near_ref[part, HEAD:], far_ref[part, HEAD:], v_ref[part])[c // 2]
            scores = masked(nt(keys_ref[rows], query) * SCALE, c, length)
            weights = jnp.exp(scores - lse)
            prob_grad = nt(value, grad)
            score_grad = (weights * (prob_grad - inner) * SCALE).astype(bf16)
            ds_ref[rows] = score_grad
            key_term = nn(score_grad, query)
            value_term = nn(weights.astype(bf16), grad)
            if h == 0:
                dk_ref[rows] = key_term
                dv_ref[rows] = value_term
            else:
                dk_ref[rows] += key_term
                dv_ref[rows] += value_term
        grad_qn = nn(keys_t_ref[...], ds_ref[...]).T
        normed = q_ref[:, cols].astype(f32) * query_factor
        u = grad_qn * qg_ref[:, cols]
        u_ref[:, cols] = u
        query_mix = query_mix + jnp.sum(u * normed, axis=1, keepdims=True)
        gain_rows.append(jnp.sum(grad_qn * normed, axis=0, keepdims=True))
    near_terms_ref[:, :HEAD] = dk_ref[:RESP]
    near_terms_ref[:, HEAD:] = dv_ref[:RESP]
    far_terms_ref[:, :HEAD] = dk_ref[RESP:PROMPT].astype(bf16)
    far_terms_ref[:, HEAD:] = dv_ref[RESP:PROMPT].astype(bf16)
    gv_ref[...] = dv_ref[PROMPT:].astype(bf16)
    grad_kn = dk_ref[PROMPT:]
    normed_key = k_ref[...].astype(f32) * key_factor
    w = grad_kn * kg_ref[...]
    w_ref[...] = w
    key_mix = jnp.sum(w * normed_key, axis=1, keepdims=True)
    gain_rows.append(jnp.sum(grad_kn * normed_key, axis=0, keepdims=True))
    tile = columns_to_tile([query_mix[:BLOCK], query_mix[BLOCK:], key_mix[:BLOCK], key_mix[BLOCK:]])
    gain_rows.append(jnp.zeros((8 - len(gain_rows), HEAD), f32))
    small_ref[...] = jnp.concatenate([tile] + gain_rows, axis=0)


def final_kernel(q_ref, k_ref, sums_ref, u_ref, w_ref, mix_ref, gq_ref, gk_ref):
    query_factor, key_factor = factors(sums_ref)
    total = mix_ref[0]
    for i in range(1, N_TENSOR):
        total = total + mix_ref[i]
    query_mix, key_mix = tile_to_columns(total)
    normed = q_ref[...].astype(f32) * query_factor
    gq_ref[...] = (
        query_factor * (u_ref[...] - normed * (query_mix / (HEADS * HEAD)))
    ).astype(bf16)
    normed_key = k_ref[...].astype(f32) * key_factor
    gk_ref[...] = (
        key_factor * (w_ref[...] - normed_key * (key_mix / (KV_HEADS * HEAD)))
    ).astype(bf16)


def call(kernel, outs, specs, scratch, flops, *args):
    return pl.pallas_call(
        kernel,
        out_shape=[jax.ShapeDtypeStruct(s, d) for s, d in outs],
        in_specs=specs,
        out_specs=[VMEM] * len(outs),
        scratch_shapes=[pltpu.VMEM(s, d) for s, d in scratch],
        compiler_params=PARAMS,
        cost_estimate=pl.CostEstimate(flops=flops, bytes_accessed=0, transcendentals=0),
    )(*args)


def after(array, *others):
    return lax.optimization_barrier((array,) + others)[0]


def swap(array, even, odd):
    pairs = [(i, i ^ (odd if i % 2 else even)) for i in range(N_TRAINER)]
    return lax.ppermute(array, TRAINER, pairs)


class Route:
    def __init__(self, me, source):
        self.me, self.source = me, source
        self.core = me & 1
        self.first = jnp.where(self.core == 0, 8, 4)
        self.last = 12 - self.first

    def pair(self, blocks):
        mine = lax.dynamic_index_in_dim(blocks, self.core, 0, keepdims=False)
        other = lax.dynamic_index_in_dim(blocks, 1 - self.core, 0, keepdims=False)
        return jnp.stack([mine, swap(other, 1, 1)])

    def four(self, pair, *earlier):
        return jnp.concatenate([pair, after(swap(pair, 8, 4), *earlier)], axis=0)

    def eight(self, four):
        return four, swap(four, 2, 2)

    def pick(self, eight, source):
        offset = source ^ self.me
        slot = bit(offset, 1) + 2 * bit(offset, self.first)
        near, far = (lax.dynamic_index_in_dim(four, slot, 0, keepdims=False) for four in eight)
        return jnp.where((offset & 2) != 0, far, near)

    def wanted(self, eight):
        there = self.me ^ self.last
        return jnp.stack([self.pick(eight, self.source(there ^ i, self.core)) for i in range(2)])

    def found(self, eight, wanted, *earlier):
        came = after(swap(wanted, 4, 8), *earlier)
        found = []
        for i in range(2):
            source = self.source(self.me ^ i, self.core)
            far = ((source ^ self.me) & self.last) != 0
            found.append(jnp.where(far, came[i], self.pick(eight, source)))
        return found

    def passed(self, found):
        return swap(found, 1, 1)


def bit(number, mask):
    return jnp.where((number & mask) != 0, 1, 0)


def on_device(
    queries,
    resp_keys,
    resp_values,
    prompt_keys,
    prompt_values,
    q_gain,
    k_gain,
    lengths,
    block_rank,
    out_grad,
):
    me = lax.axis_index(TRAINER)
    core = me & 1
    table = block_rank[0]
    ranks = jnp.arange(N_TRAINER, dtype=jnp.int32)

    def home_source(dest, b):
        return lax.dynamic_index_in_dim(table[:, b], dest, 0, keepdims=False)

    def balanced_source(dest, b):
        return jnp.sum(jnp.where(table[:, b] == dest, ranks, 0))

    query, key, value = queries[0, 0], resp_keys[0, 0], resp_values[0, 0]
    q_row, k_row = q_gain[None], k_gain[None]

    sums, pairs = call(
        stats_kernel,
        [((N_TENSOR, 8, BLOCK), f32), ((N_TRAINER, PROMPT // N_TRAINER, 2 * HEAD), bf16)],
        [VMEM] * 4,
        [],
        0,
        query,
        key,
        prompt_keys[0],
        prompt_values[0],
    )
    to_home = Route(me, home_source)
    grad_pair, sums, pairs = lax.optimization_barrier(
        (to_home.pair(out_grad.reshape(BLOCKS, BLOCK, WIDTH)), sums, pairs)
    )
    sums = lax.all_to_all(sums, "tensor", 0, 0, tiled=True)
    grad_four = to_home.four(grad_pair, sums)
    grad_four, pairs = lax.optimization_barrier((grad_four, pairs))
    grad_eight = to_home.eight(grad_four)
    pairs = lax.all_to_all(pairs, TRAINER, 0, 0, tiled=True)
    grad_wanted = to_home.wanted(grad_eight)
    pairs = after(pairs, grad_wanted).reshape(N_TRAINER // 2, 2, -1, 2 * HEAD)
    near, far = (
        lax.dynamic_index_in_dim(pairs, i, 1, keepdims=False).reshape(RESP, 2 * HEAD)
        for i in (core, 1 - core)
    )
    grad_found = to_home.found(grad_eight, grad_wanted)
    info = jnp.stack([lengths[0, 0], core])
    shared = (query, key, value, near, far, sums, q_row, k_row)
    query_n, key_list, lse, home_out = call(
        forward_kernel,
        [((RESP, WIDTH), bf16), ((KEYS, HEAD), bf16), ((8, RESP), f32), ((RESP, WIDTH), bf16)],
        [SMEM] + [VMEM] * 8,
        [((HEAD, KEYS), bf16), ((KEYS, RESP), f32), ((KEYS, RESP), bf16)],
        0,
        info,
        *shared,
    )

    to_ranks = Route(me, balanced_source)
    out_pair = to_ranks.pair(home_out.reshape(BLOCKS, BLOCK, WIDTH))
    grad_found[1], out_pair = lax.optimization_barrier((grad_found[1], out_pair))
    out_four = to_ranks.four(out_pair)
    grad_own = grad_found[0]
    grad_passed = to_home.passed(grad_found[1])

    u, w, grad_values, near_terms, far_terms, small = call(
        backward_kernel,
        [
            ((RESP, WIDTH), f32),
            ((RESP, HEAD), f32),
            ((RESP, HEAD), bf16),
            ((RESP, 2 * HEAD), f32),
            ((RESP, 2 * HEAD), bf16),
            ((16, HEAD), f32),
        ],
        [SMEM] + [VMEM] * 14,
        [
            ((HEAD, KEYS), bf16),
            ((RESP, WIDTH), bf16),
            ((KEYS, RESP), bf16),
            ((KEYS, HEAD), f32),
            ((KEYS, HEAD), f32),
        ],
        0,
        info,
        *shared,
        query_n,
        key_list,
        lse,
        home_out,
        grad_own,
        grad_passed,
    )
    out_four, small, far_terms = lax.optimization_barrier((out_four, small, far_terms))
    out_eight = to_ranks.eight(out_four)
    passed_terms = swap(far_terms, 1, 1)
    plane = ("x", "tensor")
    small = lax.all_to_all(
        jnp.broadcast_to(after(small, passed_terms)[None], (lax.axis_size(plane),) + small.shape), plane, 0, 0, tiled=True
    ).reshape(-1, N_TENSOR, 16, HEAD)
    mix = lax.dynamic_index_in_dim(small, lax.axis_index("x"), 0, keepdims=False)[:, :8]
    gains = lax.dynamic_index_in_dim(small, lax.axis_index("tensor"), 1, keepdims=False)
    gains = jnp.sum(gains[:, 8:], axis=0).reshape(-1, 2 * HEAD)
    gains = jnp.concatenate([gains, jnp.zeros_like(gains)], axis=0)
    owned = PROMPT // N_TRAINER
    terms = near_terms + passed_terms.astype(f32)
    terms = jnp.concatenate(
        [
            terms.reshape(N_TRAINER // 2, owned, 2 * HEAD),
            jnp.broadcast_to(gains[None], (N_TRAINER // 2,) + gains.shape),
        ],
        axis=1,
    ).astype(bf16)
    terms = lax.all_to_all(terms, "zlo", 0, 0, tiled=True)
    terms = jnp.sum(terms.astype(f32), axis=0)
    gains = terms[owned : owned + GAIN_ROWS]
    terms = terms[:owned].astype(bf16)
    out_wanted = to_ranks.wanted(out_eight)
    gains = after(gains, out_wanted)
    ends = ("zhi", "core")
    gains = lax.all_to_all(
        jnp.broadcast_to(gains[None], (lax.axis_size(ends),) + gains.shape), ends, 0, 0, tiled=True
    )
    gains = jnp.sum(gains, axis=0).reshape(-1)
    out_found = to_ranks.found(out_eight, out_wanted)

    out_own, out_passed = out_found[0], to_ranks.passed(after(out_found[1], gains))
    attn_out = jnp.where(
        core == 0,
        jnp.concatenate([out_own, out_passed], axis=0),
        jnp.concatenate([out_passed, out_own], axis=0),
    )
    grad_queries, grad_keys = call(
        final_kernel,
        [((RESP, WIDTH), bf16), ((RESP, HEAD), bf16)],
        [VMEM] * 6,
        [],
        0,
        query,
        key,
        sums,
        u,
        w,
        mix,
    )
    return (
        attn_out[None, None],
        grad_queries[None, None],
        grad_keys[None, None],
        grad_values[None, None],
        terms[None, :, :HEAD],
        terms[None, :, HEAD:],
        gains[:WIDTH],
        gains[WIDTH : WIDTH + HEAD],
    )


def solution(mesh):
    n_zhi = 2 if mesh.shape["prompt"] % 2 == 0 else 1
    shape = (mesh.shape["prompt"] // n_zhi, n_zhi, N_TRAINER // 2, 2, N_TENSOR)
    fine = jax.sharding.Mesh(mesh.devices.reshape(shape), PROMPTS + TRAINER + ("tensor",))
    rows = P(PROMPTS, TRAINER, None, "tensor")
    tokens = P(PROMPTS, TRAINER, "tensor")
    return jax.shard_map(
        on_device,
        mesh=fine,
        in_specs=(
            rows,
            rows,
            rows,
            tokens,
            tokens,
            P("tensor"),
            P("tensor"),
            P(PROMPTS, TRAINER),
            P(PROMPTS, None, None),
            rows,
        ),
        out_specs=(rows, rows, rows, rows, tokens, tokens, P("tensor"), P("tensor")),
        check_vma=False,
    )
```

```python
import jax
import jax.numpy as jnp
from jax import lax
from jax.experimental import pallas as pl
from jax.experimental.pallas import tpu as pltpu
from jax.sharding import PartitionSpec as P

HEAD = 128
HEADS = 20
KV_HEADS = 4
GROUP = HEADS // KV_HEADS
BLOCK = 128
BLOCKS = 2
RESP = BLOCK * BLOCKS
PROMPT = 512
KEYS = PROMPT + RESP
CHUNKS = KEYS // BLOCK
PROMPT_CHUNKS = PROMPT // BLOCK
N_TRAINER = 16
N_TENSOR = 4
PROMPTS = ("x", "zhi")
TRAINER = ("zlo", "core")
WIDTH = GROUP * HEAD
GAIN_ROWS = (GROUP + 1) // 2
SCALE = HEAD ** (-0.5)

epsilon = 1e-06
f32 = jnp.float32
bf16 = jnp.bfloat16

PARAMS = pltpu.CompilerParams(vmem_limit_bytes=24 * 1024 * 1024)
VMEM = pl.BlockSpec(memory_space=pltpu.VMEM)
SMEM = pl.BlockSpec(memory_space=pltpu.SMEM)


def nt(left, right):
    return lax.dot_general(left, right, (((1,), (1,)), ((), ())), preferred_element_type=f32)


def nn(left, right):
    return jnp.dot(left, right, preferred_element_type=f32)


def columns_to_tile(columns):
    wide = [jnp.broadcast_to(c, (BLOCK, BLOCK)).T[:1] for c in columns]
    wide.append(jnp.zeros((8 - len(columns), BLOCK), f32))
    return jnp.concatenate(wide, axis=0)


def tile_to_columns(tile):
    turned = jnp.concatenate([tile] * (BLOCK // 8), axis=0).T
    first = jnp.concatenate([turned[:, 0:1], turned[:, 1:2]], axis=0)
    second = jnp.concatenate([turned[:, 2:3], turned[:, 3:4]], axis=0)
    return first, second


def factors(sums_ref):
    total = sums_ref[0]
    for i in range(1, N_TENSOR):
        total = total + sums_ref[i]
    query_sums, key_sums = tile_to_columns(total)
    query_factor = lax.rsqrt(query_sums / (HEADS * HEAD) + epsilon)
    key_factor = lax.rsqrt(key_sums / (KV_HEADS * HEAD) + epsilon)
    return query_factor, key_factor


def stats_kernel(q_ref, k_ref, pk_ref, pv_ref, sums_ref, kv_ref):
    raw_query = q_ref[...].astype(f32)
    raw_key = k_ref[...].astype(f32)
    query_sums = jnp.sum(raw_query * raw_query, axis=1, keepdims=True)
    key_sums = jnp.sum(raw_key * raw_key, axis=1, keepdims=True)
    tile = columns_to_tile(
        [query_sums[:BLOCK], query_sums[BLOCK:], key_sums[:BLOCK], key_sums[BLOCK:]]
    )
    for i in range(N_TENSOR):
        sums_ref[i] = tile
    pair = jnp.concatenate([pk_ref[...], pv_ref[...]], axis=1)
    for i in range(N_TRAINER):
        kv_ref[i] = pair


def masked(scores, chunk, length):
    if chunk < PROMPT_CHUNKS:
        return scores
    key_pos = lax.broadcasted_iota(jnp.int32, scores.shape, 0) + (chunk - PROMPT_CHUNKS) * BLOCK
    query_pos = lax.broadcasted_iota(jnp.int32, scores.shape, 1)
    return jnp.where((key_pos <= query_pos) & (key_pos < length), scores, -1e30)


def live_column(length):
    rows = lax.broadcasted_iota(jnp.int32, (RESP, 1), 0)
    return (rows < length).astype(f32)


def forward_kernel(
    info_ref, q_ref, k_ref, v_ref, kv_ref, sums_ref, qg_ref, kg_ref,
    qn_ref, keys_ref, lse_ref, out_ref,
    values_t_ref, s_ref, p_ref,
):
    length = info_ref[0]
    query_factor, key_factor = factors(sums_ref)
    qn_ref[...] = (q_ref[...].astype(f32) * query_factor * qg_ref[...]).astype(bf16)
    keys_ref[:PROMPT] = kv_ref[:, :HEAD]
    keys_ref[PROMPT:] = (k_ref[...].astype(f32) * key_factor * kg_ref[...]).astype(bf16)
    values_t_ref[:, :PROMPT] = kv_ref[:, HEAD:].astype(f32).T.astype(bf16)
    values_t_ref[:, PROMPT:] = v_ref[...].astype(f32).T.astype(bf16)
    live = live_column(length)
    for h in range(GROUP):
        cols = slice(h * HEAD, (h + 1) * HEAD)
        query = qn_ref[:, cols]
        top = None
        for c in range(CHUNKS):
            rows = slice(c * BLOCK, (c + 1) * BLOCK)
            scores = masked(nt(keys_ref[rows], query) * SCALE, c, length)
            s_ref[rows] = scores
            most = jnp.max(scores, axis=0, keepdims=True)
            top = most if top is None else jnp.maximum(top, most)
        total = jnp.zeros_like(top)
        for c in range(CHUNKS):
            rows = slice(c * BLOCK, (c + 1) * BLOCK)
            grown = jnp.exp(s_ref[rows] - top)
            s_ref[rows] = grown
            total = total + jnp.sum(grown, axis=0, keepdims=True)
        share = 1.0 / total
        for c in range(CHUNKS):
            rows = slice(c * BLOCK, (c + 1) * BLOCK)
            p_ref[rows] = (s_ref[rows] * share).astype(bf16)
        lse_ref[h : h + 1] = top + jnp.log(total)
        attended = nn(values_t_ref[...], p_ref[...]).T
        out_ref[:, cols] = (attended * live).astype(bf16)
    lse_ref[GROUP:] = jnp.zeros((8 - GROUP, RESP), f32)


def backward_kernel(
    info_ref, q_ref, k_ref, v_ref, kv_ref, sums_ref, qg_ref, kg_ref,
    qn_ref, keys_ref, lse_ref, out_ref, own_ref, passed_ref,
    u_ref, w_ref, gv_ref, terms_ref, mix_ref, gain_ref,
    keys_t_ref, grad_ref, ds_ref, dk_ref, dv_ref,
):
    length = info_ref[0]
    query_factor, key_factor = factors(sums_ref)
    keys_t_ref[...] = keys_ref[...].astype(f32).T.astype(bf16)
    live = live_column(length).astype(bf16)
    swapped = info_ref[1] != 0
    first = jnp.where(swapped, passed_ref[...], own_ref[...])
    second = jnp.where(swapped, own_ref[...], passed_ref[...])
    grad_ref[:BLOCK] = first * live[:BLOCK]
    grad_ref[BLOCK:] = second * live[BLOCK:]
    query_mix = jnp.zeros((RESP, 1), f32)
    gain_rows = []
    for h in range(GROUP):
        cols = slice(h * HEAD, (h + 1) * HEAD)
        query = qn_ref[:, cols]
        grad = grad_ref[:, cols]
        inner = (grad.astype(f32) * out_ref[:, cols].astype(f32)).T
        inner = jnp.sum(inner, axis=0, keepdims=True)
        lse = lse_ref[h : h + 1]
        for c in range(CHUNKS):
            rows = slice(c * BLOCK, (c + 1) * BLOCK)
            if c < PROMPT_CHUNKS:
                value = kv_ref[rows, HEAD:]
            else:
                value = v_ref[(c - PROMPT_CHUNKS) * BLOCK : (c - PROMPT_CHUNKS + 1) * BLOCK]
            scores = masked(nt(keys_ref[rows], query) * SCALE, c, length)
            weights = jnp.exp(scores - lse)
            prob_grad = nt(value, grad)
            score_grad = (weights * (prob_grad - inner) * SCALE).astype(bf16)
            ds_ref[rows] = score_grad
            key_term = nn(score_grad, query)
            value_term = nn(weights.astype(bf16), grad)
            if h == 0:
                dk_ref[rows] = key_term
                dv_ref[rows] = value_term
            else:
                dk_ref[rows] += key_term
                dv_ref[rows] += value_term
        grad_qn = nn(keys_t_ref[...], ds_ref[...]).T
        normed = q_ref[:, cols].astype(f32) * query_factor
        u = grad_qn * qg_ref[:, cols]
        u_ref[:, cols] = u
        query_mix = query_mix + jnp.sum(u * normed, axis=1, keepdims=True)
        gain_rows.append(jnp.sum(grad_qn * normed, axis=0, keepdims=True))
    terms_ref[:, :HEAD] = dk_ref[:PROMPT]
    terms_ref[:, HEAD:] = dv_ref[:PROMPT]
    gv_ref[...] = dv_ref[PROMPT:].astype(bf16)
    grad_kn = dk_ref[PROMPT:]
    normed_key = k_ref[...].astype(f32) * key_factor
    w = grad_kn * kg_ref[...]
    w_ref[...] = w
    key_mix = jnp.sum(w * normed_key, axis=1, keepdims=True)
    gain_rows.append(jnp.sum(grad_kn * normed_key, axis=0, keepdims=True))
    gains = jnp.concatenate(
        [jnp.concatenate(gain_rows[i : i + 2], axis=1) for i in range(0, GROUP + 1, 2)], axis=0
    )
    gain_ref[...] = jnp.concatenate(
        [gains, jnp.zeros((8 - GAIN_ROWS, 2 * HEAD), f32)], axis=0
    )
    tile = columns_to_tile([query_mix[:BLOCK], query_mix[BLOCK:], key_mix[:BLOCK], key_mix[BLOCK:]])
    for i in range(N_TENSOR):
        mix_ref[i] = tile


def final_kernel(q_ref, k_ref, sums_ref, u_ref, w_ref, mix_ref, gq_ref, gk_ref):
    query_factor, key_factor = factors(sums_ref)
    total = mix_ref[0]
    for i in range(1, N_TENSOR):
        total = total + mix_ref[i]
    query_mix, key_mix = tile_to_columns(total)
    normed = q_ref[...].astype(f32) * query_factor
    gq_ref[...] = (
        query_factor * (u_ref[...] - normed * (query_mix / (HEADS * HEAD)))
    ).astype(bf16)
    normed_key = k_ref[...].astype(f32) * key_factor
    gk_ref[...] = (
        key_factor * (w_ref[...] - normed_key * (key_mix / (KV_HEADS * HEAD)))
    ).astype(bf16)


def call(kernel, outs, specs, scratch, flops, *args):
    return pl.pallas_call(
        kernel,
        out_shape=[jax.ShapeDtypeStruct(s, d) for s, d in outs],
        in_specs=specs,
        out_specs=[VMEM] * len(outs),
        scratch_shapes=[pltpu.VMEM(s, d) for s, d in scratch],
        compiler_params=PARAMS,
        cost_estimate=pl.CostEstimate(flops=flops, bytes_accessed=0, transcendentals=0),
    )(*args)


def after(array, *others):
    return lax.optimization_barrier((array,) + others)[0]


def swap(array, even, odd):
    pairs = [(i, i ^ (odd if i % 2 else even)) for i in range(N_TRAINER)]
    return lax.ppermute(array, TRAINER, pairs)


class Route:
    def __init__(self, me, source):
        self.me, self.source = me, source
        self.core = me & 1
        self.first = jnp.where(self.core == 0, 8, 4)
        self.last = 12 - self.first

    def pair(self, blocks):
        mine = lax.dynamic_index_in_dim(blocks, self.core, 0, keepdims=False)
        other = lax.dynamic_index_in_dim(blocks, 1 - self.core, 0, keepdims=False)
        return jnp.stack([mine, swap(other, 1, 1)])

    def four(self, pair, *earlier):
        return jnp.concatenate([pair, after(swap(pair, 8, 4), *earlier)], axis=0)

    def eight(self, four):
        return four, swap(four, 2, 2)

    def pick(self, eight, source):
        offset = source ^ self.me
        slot = bit(offset, 1) + 2 * bit(offset, self.first)
        near, far = (lax.dynamic_index_in_dim(four, slot, 0, keepdims=False) for four in eight)
        return jnp.where((offset & 2) != 0, far, near)

    def wanted(self, eight):
        there = self.me ^ self.last
        return jnp.stack([self.pick(eight, self.source(there ^ i, self.core)) for i in range(2)])

    def found(self, eight, wanted, *earlier):
        came = after(swap(wanted, 4, 8), *earlier)
        found = []
        for i in range(2):
            source = self.source(self.me ^ i, self.core)
            far = ((source ^ self.me) & self.last) != 0
            found.append(jnp.where(far, came[i], self.pick(eight, source)))
        return found

    def passed(self, found):
        return swap(found, 1, 1)


def bit(number, mask):
    return jnp.where((number & mask) != 0, 1, 0)


def on_device(
    queries,
    resp_keys,
    resp_values,
    prompt_keys,
    prompt_values,
    q_gain,
    k_gain,
    lengths,
    block_rank,
    out_grad,
):
    me = lax.axis_index(TRAINER)
    core = me & 1
    table = block_rank[0]
    ranks = jnp.arange(N_TRAINER, dtype=jnp.int32)

    def home_source(dest, b):
        return lax.dynamic_index_in_dim(table[:, b], dest, 0, keepdims=False)

    def balanced_source(dest, b):
        return jnp.sum(jnp.where(table[:, b] == dest, ranks, 0))

    query, key, value = queries[0, 0], resp_keys[0, 0], resp_values[0, 0]
    q_row, k_row = q_gain[None], k_gain[None]

    sums, pairs = call(
        stats_kernel,
        [((N_TENSOR, 8, BLOCK), f32), ((N_TRAINER, PROMPT // N_TRAINER, 2 * HEAD), bf16)],
        [VMEM] * 4,
        [],
        0,
        query,
        key,
        prompt_keys[0],
        prompt_values[0],
    )
    to_home = Route(me, home_source)
    grad_pair, sums, pairs = lax.optimization_barrier(
        (to_home.pair(out_grad.reshape(BLOCKS, BLOCK, WIDTH)), sums, pairs)
    )
    sums = lax.all_to_all(sums, "tensor", 0, 0, tiled=True)
    grad_four = to_home.four(grad_pair, sums)
    grad_four, pairs = lax.optimization_barrier((grad_four, pairs))
    grad_eight = to_home.eight(grad_four)
    pairs = lax.all_to_all(pairs, TRAINER, 0, 0, tiled=True).reshape(PROMPT, 2 * HEAD)
    grad_wanted = to_home.wanted(grad_eight)
    pairs = after(pairs, grad_wanted)
    grad_found = to_home.found(grad_eight, grad_wanted)
    info = jnp.stack([lengths[0, 0], core])
    shared = (query, key, value, pairs, sums, q_row, k_row)
    query_n, key_list, lse, home_out = call(
        forward_kernel,
        [((RESP, WIDTH), bf16), ((KEYS, HEAD), bf16), ((8, RESP), f32), ((RESP, WIDTH), bf16)],
        [SMEM] + [VMEM] * 7,
        [((HEAD, KEYS), bf16), ((KEYS, RESP), f32), ((KEYS, RESP), bf16)],
        0,
        info,
        *shared,
    )

    to_ranks = Route(me, balanced_source)
    out_pair = to_ranks.pair(home_out.reshape(BLOCKS, BLOCK, WIDTH))
    grad_found[1], out_pair = lax.optimization_barrier((grad_found[1], out_pair))
    out_four = to_ranks.four(out_pair)
    grad_own = grad_found[0]
    grad_passed = to_home.passed(grad_found[1])

    u, w, grad_values, terms, mix, gains = call(
        backward_kernel,
        [
            ((RESP, WIDTH), f32),
            ((RESP, HEAD), f32),
            ((RESP, HEAD), bf16),
            ((PROMPT, 2 * HEAD), f32),
            ((N_TENSOR, 8, BLOCK), f32),
            ((8, 2 * HEAD), f32),
        ],
        [SMEM] + [VMEM] * 13,
        [
            ((HEAD, KEYS), bf16),
            ((RESP, WIDTH), bf16),
            ((KEYS, RESP), bf16),
            ((KEYS, HEAD), f32),
            ((KEYS, HEAD), f32),
        ],
        0,
        info,
        *shared,
        query_n,
        key_list,
        lse,
        home_out,
        grad_own,
        grad_passed,
    )
    out_four, gains, terms = lax.optimization_barrier((out_four, gains, terms))
    out_eight = to_ranks.eight(out_four)
    owned = PROMPT // N_TRAINER
    terms = jnp.concatenate(
        [
            terms.reshape(N_TRAINER, owned, 2 * HEAD),
            jnp.broadcast_to(gains[None], (N_TRAINER,) + gains.shape),
        ],
        axis=1,
    ).reshape(N_TRAINER // 2, 2, owned + gains.shape[0], 2 * HEAD)
    near, far = (
        lax.dynamic_index_in_dim(terms, i, 1, keepdims=False) for i in (core, 1 - core)
    )
    terms = (near + swap(far.astype(bf16), 1, 1).astype(f32)).astype(bf16)
    mix = lax.all_to_all(mix, "tensor", 0, 0, tiled=True)
    terms = lax.all_to_all(after(terms, mix), "zlo", 0, 0, tiled=True)
    terms = jnp.sum(terms.astype(f32), axis=0)
    gains = terms[owned : owned + GAIN_ROWS]
    terms = terms[:owned].astype(bf16)
    out_wanted = to_ranks.wanted(out_eight)
    gains = after(gains, out_wanted)
    gains = lax.all_to_all(
        jnp.broadcast_to(gains[None], (lax.axis_size(PROMPTS),) + gains.shape),
        PROMPTS,
        0,
        0,
        tiled=True,
    )
    gains = jnp.sum(gains, axis=0).reshape(-1)
    out_found = to_ranks.found(out_eight, out_wanted)

    out_own, out_passed = out_found[0], after(to_ranks.passed(out_found[1]), gains)
    attn_out = jnp.where(
        core == 0,
        jnp.concatenate([out_own, out_passed], axis=0),
        jnp.concatenate([out_passed, out_own], axis=0),
    )
    grad_queries, grad_keys = call(
        final_kernel,
        [((RESP, WIDTH), bf16), ((RESP, HEAD), bf16)],
        [VMEM] * 6,
        [],
        0,
        query,
        key,
        sums,
        u,
        w,
        mix,
    )
    return (
        attn_out[None, None],
        grad_queries[None, None],
        grad_keys[None, None],
        grad_values[None, None],
        terms[None, :, :HEAD],
        terms[None, :, HEAD:],
        gains[:WIDTH],
        gains[WIDTH : WIDTH + HEAD],
    )


def solution(mesh):
    n_zhi = 2 if mesh.shape["prompt"] % 2 == 0 else 1
    shape = (mesh.shape["prompt"] // n_zhi, n_zhi, N_TRAINER // 2, 2, N_TENSOR)
    fine = jax.sharding.Mesh(mesh.devices.reshape(shape), PROMPTS + TRAINER + ("tensor",))
    rows = P(PROMPTS, TRAINER, None, "tensor")
    tokens = P(PROMPTS, TRAINER, "tensor")
    return jax.shard_map(
        on_device,
        mesh=fine,
        in_specs=(
            rows,
            rows,
            rows,
            tokens,
            tokens,
            P("tensor"),
            P("tensor"),
            P(PROMPTS, TRAINER),
            P(PROMPTS, None, None),
            rows,
        ),
        out_specs=(rows, rows, rows, rows, tokens, tokens, P("tensor"), P("tensor")),
        check_vma=False,
    )
```
